32 devices in a mesh: groups: 2 (over y), lon: 4 (over z), lat: 2 (over x), ch: 2 (over core).
Axes of the slice: x: 2, y: 2, z: 4, core: 2. Of those that a mesh axis runs over, the one named last changes fastest.
Arguments:
- features: float32 [12288, 256], P(('groups', 'lon', 'lat'), 'ch'), parts along dimension 0, may hold values from -6 to 6
- blocks: float32 [48, 3, 128, 128], P(('lon', 'lat')), may hold values from -0.3125 to 0.3125
- sources: int32 [48, 3], P(('lon', 'lat')), may hold values from 0 to 9, as said below
- live: int32 [8], P(('lon', 'lat')), may hold values from 4 to 6, as said below
- weights: float32 [4, 256, 256], P(None, None, 'ch'), may hold values from -0.1875 to 0.1875
- cotangent: float32 [12288, 256], P(('groups', 'lon', 'lat'), 'ch'), parts along dimension 0, may hold values from -6 to 6
Outputs:
- output: float32 [12288, 256], P(('groups', 'lon', 'lat'), 'ch'), parts along dimension 0
- input_grad: float32 [12288, 256], P(('groups', 'lon', 'lat'), 'ch'), parts along dimension 0
- weight_grad: float32 [8, 256, 256], P('groups', None, 'ch'), parts along dimension 0
The draws below stay inside these ranges and needn't reach their ends.
There are 2 independent parts, one for each index of `groups`. The reference program is written for one: setup_inputs(seed, part) draws one part's arguments, and reference() takes and returns one part's arrays. A program takes and returns all parts, laid end to end along the dimension named above; an argument that names none is the same for every part. Nothing has to cross between parts.
Inputs may be any that keep to these rules, and one draw needn't show every extreme that they name: `sources`: on tile t of every sector and band, block 0 reads tile t itself; for t < 4, block 1 reads extended entry 6 + t; other blocks read any entry of the extended list. Bands other than the first and last are fully live; in those two, sector 0 holds 6 live tiles, sector 1 holds 4, and the others 6 - 2 to 6.
All inputs are finite; a program needn't handle non-finite values.
Results may differ from the reference program's by a relative error of at most 0.0003.
Values sent between devices are 32-bit elements; how exact they have to be, the bound alone decides.
A program may use at most 64 MiB of HBM per device.

```python
import jax
import jax.numpy as jnp
from jax import lax

CIN = 256
COUT = 256
CHEB = 4
TILE = 128
SLOTS = 3
TILES = 6
NDEV = 8
NTILES = 48
NPIX = 6144
N_LON = 4
N_LAT = 2


def draw_sources(key, part):
    rows = (jnp.arange(NTILES) % TILES).astype(jnp.int32)
    first_key, second_key = jax.random.split(jax.random.fold_in(key, 11))
    second = jnp.where(rows < 4, TILES + rows, jax.random.randint(first_key, (NTILES,), 0, TILES))
    third = jax.random.randint(second_key, (NTILES,), 0, TILES + 4)
    return jnp.stack([rows, second.astype(jnp.int32), third.astype(jnp.int32)], axis=1).astype(jnp.int32)


def draw_live(key, part):
    index = jnp.arange(NDEV).astype(jnp.int32)
    band = index % N_LAT
    sector = index // N_LAT
    polar = (band == 0) | (band == N_LAT - 1)
    drawn = jax.random.randint(jax.random.fold_in(key, 23), (NDEV,), TILES - 2, TILES + 1)
    drawn = jnp.where(sector == 0, TILES, jnp.where(sector == 1, TILES - 2, drawn))
    return jnp.where(polar, drawn, TILES).astype(jnp.int32)


def levels(rng, extent, shards, low, largest):
    loudness = 1.0
    for dim, blocks in shards:
        draws = jax.random.uniform(jax.random.fold_in(jax.random.fold_in(rng, 6), dim), (blocks,), jnp.float32, low / len(shards), largest / len(shards))
        loudness = loudness * jnp.repeat(jnp.exp(draws), extent[dim] // blocks).reshape((-1,) + (1,) * (len(extent) - 1 - dim))
    return loudness


def centred(rng, extent, scale, limit, cuts=(), kind=jnp.bfloat16):
    gain = levels(rng, extent, cuts, -0.22, 0.18) if cuts else 1.0
    values = jax.random.normal(rng, extent, jnp.float32) * scale * gain
    return jnp.minimum(jnp.maximum(values, -limit), limit).astype(kind)


def setup_inputs(seed: int = 0, part: int = 0) -> dict:
    streams_of = jax.random.split(jax.random.key(seed), 7)
    part_keys = jax.random.split(jax.random.fold_in(streams_of[6], part), 7)
    features = centred(part_keys[0], (NPIX, CIN), 1.0, 6.0, ((0, 8), (1, 2)), jnp.float32)
    blocks = centred(streams_of[1], (NTILES, SLOTS, TILE, TILE), (SLOTS * TILE) ** -0.5, 0.3125, ((0, 8),), jnp.float32)
    sources = draw_sources(jax.random.fold_in(streams_of[6], 71), part)
    live = draw_live(jax.random.fold_in(streams_of[6], 71), part)
    weights = centred(streams_of[4], (CHEB, CIN, COUT), (CHEB * CIN) ** -0.5, 0.1875, ((2, 2),), jnp.float32)
    cotangent = centred(part_keys[5], (NPIX, COUT), 1.0, 6.0, ((0, 8), (1, 2)), jnp.float32)
    return dict(features=features, blocks=blocks, sources=sources, live=live, weights=weights, cotangent=cotangent)


highest_accuracy = lax.Precision.HIGHEST


def extend(pixel_field):
    west = jnp.roll(pixel_field[:, :, 1], 1, axis=0)
    east = jnp.roll(pixel_field[:, :, 0], -1, axis=0)
    zero = jnp.zeros_like(pixel_field[:, :1, 0])
    south = jnp.concatenate([zero, pixel_field[:, :-1, 3]], axis=1)
    north = jnp.concatenate([pixel_field[:, 1:, 2], zero], axis=1)
    return jnp.concatenate([pixel_field, jnp.stack([west, east, south, north], axis=2)], axis=2)


def forward_apply(pixel_field, blocks, sources, keep_mask):
    width = pixel_field.shape[-1]
    grid = pixel_field.reshape(N_LON, N_LAT, TILES, TILE, width)
    extended = extend(grid).reshape(NDEV, TILES + 4, TILE, width)

    def one_device(items):
        ext_tiles, shard_block_list, dev_sources = items
        selected_entries = ext_tiles[dev_sources]
        return jnp.einsum('dfox,dfxk->dok', shard_block_list, selected_entries, precision=highest_accuracy)

    result = lax.map(one_device, (extended, blocks, sources))
    return result * keep_mask


def adjoint_apply(pixel_field, blocks, sources, keep_mask):
    width = pixel_field.shape[-1]
    positions = jnp.arange(TILES + 4).astype(jnp.int32)

    def one_device(items):
        shard_pixel_field, shard_block_list, dev_sources = items
        share_amount = jnp.einsum('yerj,yri->yeji', shard_block_list, shard_pixel_field, precision=highest_accuracy)
        selector = (dev_sources[:, :, None] == positions[None, None, :]).astype(jnp.float32)
        return jnp.einsum('tse,tsbc->ebc', selector, share_amount, precision=highest_accuracy)

    spread = lax.map(one_device, (pixel_field * keep_mask, blocks, sources))
    spread = spread.reshape(N_LON, N_LAT, TILES + 4, TILE, width)
    local = spread[:, :, :TILES]
    halo = spread[:, :, TILES:]
    zero = jnp.zeros_like(halo[:, :1, 0])
    first = jnp.roll(halo[:, :, 1], 1, axis=0)
    second = jnp.roll(halo[:, :, 0], -1, axis=0)
    third = jnp.concatenate([zero, halo[:, :-1, 3]], axis=1)
    fourth = jnp.concatenate([halo[:, 1:, 2], zero], axis=1)
    added = jnp.stack([first, second, third, fourth], axis=2)
    local = jnp.concatenate([local[:, :, :4] + added, local[:, :, 4:]], axis=2)
    return local.reshape(NDEV, TILES, TILE, width) * keep_mask


def reference(features, blocks, sources, live, weights, cotangent):
    keep_mask = (jnp.arange(TILES)[None, :] < live[:, None]).astype(jnp.float32)[:, :, None, None]
    tile_blocks = blocks.reshape(NDEV, TILES, SLOTS, TILE, TILE)
    tile_sources = sources.reshape(NDEV, TILES, SLOTS)
    start = features.reshape(NDEV, TILES, TILE, CIN) * keep_mask
    terms = [start]
    terms.append(forward_apply(start, tile_blocks, tile_sources, keep_mask))
    for order in range(2, CHEB):
        terms.append(2.0 * forward_apply(terms[-1], tile_blocks, tile_sources, keep_mask) - terms[-2])
    output = jnp.zeros((NDEV, TILES, TILE, COUT), jnp.float32)
    for order in range(CHEB):
        output = output + jnp.einsum('ntpc,co->ntpo', terms[order], weights[order], precision=highest_accuracy)
    goal = cotangent.reshape(NDEV, TILES, TILE, COUT) * keep_mask
    scale = float(NPIX) ** -0.5
    grads = jnp.stack([jnp.einsum('ntpc,ntpo->co', terms[order], goal, precision=highest_accuracy) * scale for order in range(CHEB)])
    adjoint = [jnp.einsum('ntpo,co->ntpc', goal, weights[order], precision=highest_accuracy) for order in range(CHEB)]
    for order in range(CHEB - 1, 1, -1):
        adjoint[order - 1] = adjoint[order - 1] + 2.0 * adjoint_apply(adjoint[order], tile_blocks, tile_sources, keep_mask)
        adjoint[order - 2] = adjoint[order - 2] - adjoint[order]
    adjoint[0] = adjoint[0] + adjoint_apply(adjoint[1], tile_blocks, tile_sources, keep_mask)
    input_grad = (adjoint[0] * keep_mask).reshape(NPIX, CIN)
    return output.reshape(NPIX, COUT), input_grad, grads
```

```python
import functools

import jax
import jax.numpy as jnp
from jax import lax
from jax.experimental import pallas as pl
from jax.experimental.pallas import tpu as pltpu
from jax.sharding import PartitionSpec as P

CHEB = 4
TILE = 128
TILES = 6
ROWS = TILE * TILES
MESH = pl.DeviceIdType.MESH
F32 = jnp.float32
BF16 = jnp.bfloat16


def dot(a, b):
    return jnp.dot(a, b, preferred_element_type=F32)


def split(x):
    hi = x.astype(BF16)
    return hi, (x - hi.astype(F32)).astype(BF16)


def kernel(
    n_lon, n_lat, own_lon, scale,
    feat, blocks, src, live, w, cot,
    out, ig, wg,
    fx, f_hi, f_lo, ft_hi, ft_lo, w_hl, wt_hh, wt_lo, bb, bt,
    u, b, s, s_hl, ext, loc, free, sp,
    recv_f, recv_s, ig_acc, ig_send, ig_recv,
    wg_part, rx, wg_x, rz, wg_sum,
    fx_sem, hf_send, hf_recv, hs_send, hs_recv, ig_ssem, ig_rsem,
    rx_send, rx_recv, rz_send, rz_recv, az_send, az_recv, ax_send, ax_recv,
):
    part = 256 // n_lat
    piece = part // own_lon
    ch = lax.axis_index("ch")
    lon = lax.axis_index("lon")
    lat = lax.axis_index("lat")
    west = lax.rem(lon + n_lon - 1, n_lon)
    east = lax.rem(lon + 1, n_lon)
    mine = pl.ds(pl.multiple_of(ch * 128, 128), 128)
    other = pl.ds(pl.multiple_of((1 - ch) * 128, 128), 128)

    def rows(t):
        return pl.ds(t * TILE, TILE)

    def mask(t):
        return (t < live[0]).astype(F32)

    def remote(a, d, ssem, rsem, dev):
        return pltpu.make_async_remote_copy(
            src_ref=a, dst_ref=d, send_sem=ssem, recv_sem=rsem, device_id=dev, device_id_type=MESH
        )

    barrier = pltpu.get_barrier_semaphore()
    pl.semaphore_signal(barrier, inc=1, device_id={"ch": 1 - ch}, device_id_type=MESH)
    for d in range(1, n_lat):
        pl.semaphore_signal(barrier, inc=1, device_id={"lat": lax.rem(lat + d, n_lat)}, device_id_type=MESH)

    @pl.loop(1, n_lon)
    def _(d):
        pl.semaphore_signal(barrier, inc=1, device_id={"lon": lax.rem(lon + d, n_lon)}, device_id_type=MESH)

    has_south = lat > 0
    has_north = lat < n_lat - 1

    def halo_f(i, v):
        return (
            (None, remote(v.at[rows(1)], recv_f.at[i, 0], hf_send.at[i, 0], hf_recv.at[i, 0], {"lon": east})),
            (None, remote(v.at[rows(0)], recv_f.at[i, 1], hf_send.at[i, 1], hf_recv.at[i, 1], {"lon": west})),
            (has_north, remote(v.at[rows(3)], recv_f.at[i, 2], hf_send.at[i, 2], hf_recv.at[i, 2], {"lat": lat + 1})),
            (has_south, remote(v.at[rows(2)], recv_f.at[i, 3], hf_send.at[i, 3], hf_recv.at[i, 3], {"lat": lat - 1})),
        )

    def halo_s(i):
        return (
            (None, remote(sp.at[i, 0], recv_s.at[i, 1], hs_send.at[i, 0], hs_recv.at[i, 1], {"lon": west})),
            (None, remote(sp.at[i, 1], recv_s.at[i, 0], hs_send.at[i, 1], hs_recv.at[i, 0], {"lon": east})),
            (has_south, remote(sp.at[i, 2], recv_s.at[i, 3], hs_send.at[i, 2], hs_recv.at[i, 3], {"lat": lat - 1})),
            (has_north, remote(sp.at[i, 3], recv_s.at[i, 2], hs_send.at[i, 3], hs_recv.at[i, 2], {"lat": lat + 1})),
        )

    def on(condition, action):
        if condition is None:
            action()
        else:
            pl.when(condition)(action)

    def start(copies):
        for condition, copy in copies:
            on(condition, copy.start)

    def sent(copies):
        for condition, copy in copies:
            on(condition, copy.wait_send)

    def landed(i, buffer, sems):
        for j, condition in ((0, None), (1, None), (2, has_south), (3, has_north)):
            at = buffer.at[i, j]
            on(condition, remote(at, at, hf_send.at[i, j], sems.at[i, j], {"lon": east}).wait_recv)

    def put_s(k, t, value):
        s[k, rows(t), :] = value
        hi, lo = split(value)
        s_hl[k, rows(t), 0:128] = hi
        s_hl[k, rows(t), 128:256] = lo

    def spread(i):
        for t in range(TILES):
            a = s_hl[i, rows(t), :]
            low = jnp.concatenate([a[:, 0:128], jnp.zeros((128, 128), BF16)], axis=1)
            r = dot(bt[t], jnp.concatenate([a, low], axis=0))
            share = r[:, 0:128] + r[:, 128:256]
            loc[t] = share[0:128]
            if t < 4:
                loc[6 + t] = share[128:256]
            else:
                free[2 + t] = share[128:256]
            free[t] = share[256:384]

        def gathered(e):
            total = loc[e]
            for f in range(8):
                entry = src[f, 2] if f < 6 else src[f - 2, 1]
                total = total + (entry == e).astype(F32) * free[f]
            return total

        @pl.loop(6, 10)
        def _(e):
            sp[i, e - 6] = gathered(e)

        start(halo_s(i))

        @pl.loop(0, 6)
        def _(e):
            loc[e] = gathered(e)

    def finish_s(i):
        landed(i, recv_s, hs_recv)
        for t in range(TILES):
            total = loc[t]
            if t < 4:
                total = total + recv_s[i, t]
            total = total * mask(t)
            if i > 0:
                total = 2.0 * total - s[i - 1, rows(t), :]
            put_s(i + 1, t, total)

    def put_ext(t, value):
        hi, lo = split(value)
        ext[t, :, 0:128] = hi
        ext[t, :, 128:256] = lo

    def apply(t):
        x = jnp.concatenate([ext[src[t, 0]], ext[src[t, 1]], ext[src[t, 2]]], axis=0)
        r = dot(bb[t], x)
        return (r[0:128, 0:128] + (r[0:128, 128:256] + r[128:256, 0:128])) * mask(t)

    def halo_in(i):
        landed(i, recv_f, hf_recv)
        for j in range(4):
            put_ext(6 + j, recv_f[i, j])

    def wg_partial(k):
        a = s_hl[k]
        r = dot(ft_hi[...], a)
        r = (r[:, 0:128] + r[:, 128:256] + dot(ft_lo[...], a[:, 0:128])) * scale
        wg_part[k, mine, :] = r[0:128]
        wg_part[k, other, :] = r[128:256]
        for d in range(1, n_lat):
            x_copy(k, d).start()

    def part_of(index):
        return pl.ds(pl.multiple_of(index * part, 8), part)

    def piece_of(index):
        return pl.ds(pl.multiple_of(index * piece, 8), piece)

    def x_copy(k, d):
        to = lax.rem(lat + d, n_lat)
        return remote(wg_part.at[k, part_of(to)], rx.at[k, d - 1], rx_send.at[k, d - 1], rx_recv.at[k, d - 1], {"lat": to})

    def z_copy(k, d):
        to = lax.rem(lon + d, n_lon)
        return to, remote(wg_x.at[k, piece_of(to)], rz.at[k, d - 1], rz_send.at[k, d - 1], rz_recv.at[k, d - 1], {"lon": to})

    def final_piece(k, owner):
        return wg_sum.at[k, pl.ds(pl.multiple_of(lat * part + owner * piece, 8), piece)]

    def az_copy(k, d):
        at = final_piece(k, lon)
        return remote(at, at, az_send.at[k, d - 1], az_recv.at[k, d - 1], {"lon": lax.rem(lon + d, n_lon)})

    def ax_copy(k, d):
        at = wg_sum.at[k, part_of(lat)]
        return remote(at, at, ax_send.at[k, d - 1], ax_recv.at[k, d - 1], {"lat": lax.rem(lat + d, n_lat)})

    def each_lon(body):
        if n_lon <= 4:
            for d in range(1, n_lon):
                body(d)
        else:
            pl.loop(1, n_lon)(body)

    everyone = own_lon == n_lon
    is_owner = None if everyone else lon < own_lon

    def owner_only(index, action):
        on(None if everyone else index < own_lon, action)

    def wg_lat(k):
        total = wg_part[k, part_of(lat), :]
        for d in range(1, n_lat):
            x_copy(k, d).wait_recv()
            total = total + rx[k, d - 1]
        wg_x[k] = total

        def send(d):
            to, copy = z_copy(k, d)
            owner_only(to, copy.start)

        each_lon(send)

    def wg_lon(k):
        def total_up():
            each_lon(lambda d: z_copy(k, d)[1].wait_recv())
            total = wg_x[k, piece_of(lon), :]
            if n_lon <= 4:
                for d in range(1, n_lon):
                    total = total + rz[k, d - 1]
            else:
                total = lax.fori_loop(1, n_lon, lambda d, t: t + rz[k, d - 1], total)
            wg_sum[k, pl.ds(pl.multiple_of(lat * part + lon * piece, 8), piece), :] = total
            each_lon(lambda d: az_copy(k, d).start())

        on(is_owner, total_up)

    def wg_back(k):
        def take(d):
            owner = lax.rem(lon + n_lon - d, n_lon)

            def wait():
                at = final_piece(k, owner)
                remote(at, at, az_send.at[k, d - 1], az_recv.at[k, d - 1], {"lon": east}).wait_recv()

            owner_only(owner, wait)

        each_lon(take)
        for d in range(1, n_lat):
            ax_copy(k, d).start()

    def wg_done(k):
        for d in range(1, n_lat):
            at = wg_sum.at[k, part_of(lax.rem(lat + n_lat - d, n_lat))]
            remote(at, at, ax_send.at[k, d - 1], ax_recv.at[k, d - 1], {"lon": east}).wait_recv()
        wg[k] = wg_sum[k]

    def wg_sent(k):
        for d in range(1, n_lat):
            x_copy(k, d).wait_send()
            ax_copy(k, d).wait_send()

        def wait(d):
            to, copy = z_copy(k, d)
            owner_only(to, copy.wait_send)

        each_lon(wait)
        on(is_owner, lambda: each_lon(lambda d: az_copy(k, d).wait_send()))

    def ig_copy(i):
        return remote(ig_send.at[i], ig_recv.at[i], ig_ssem.at[i], ig_rsem.at[i], {"ch": 1 - ch})

    def ig_term(k, t):
        a = s_hl[k, rows(t), :]
        return dot(a, wt_hh[k]) + dot(a[:, 0:128], wt_lo[k])

    for t in range(TILES):
        for j in range(3):
            hi, lo = split(blocks[t, j].T)
            bt[t, j * 128:(j + 1) * 128, 0:128] = hi
            bt[t, j * 128:(j + 1) * 128, 128:256] = lo
        put_s(0, t, cot[rows(t), :] * mask(t))

    @pl.when(jnp.logical_not(has_south))
    def _():
        for i in range(3):
            recv_f[i, 2] = jnp.zeros((128, 128), F32)
            recv_s[i, 2] = jnp.zeros((128, 128), F32)

    @pl.when(jnp.logical_not(has_north))
    def _():
        for i in range(3):
            recv_f[i, 3] = jnp.zeros((128, 128), F32)
            recv_s[i, 3] = jnp.zeros((128, 128), F32)

    pl.semaphore_wait(barrier, (n_lat - 1) + (n_lon - 1) + 1)
    feat_copy = remote(feat, fx, fx_sem.at[0], fx_sem.at[1], {"ch": 1 - ch})
    feat_copy.start()
    spread(0)

    for k in range(CHEB):
        for half, at in ((0, mine), (1, other)):
            value = w[k, at, :]
            hi, lo = split(value)
            w_hl[k, half * 128:(half + 1) * 128, 0:128] = hi
            w_hl[k, half * 128:(half + 1) * 128, 128:256] = lo
            hi, lo = split(value.T)
            wt_hh[k, 0:128, half * 128:(half + 1) * 128] = hi
            wt_hh[k, 128:256, half * 128:(half + 1) * 128] = hi
            wt_lo[k, :, half * 128:(half + 1) * 128] = lo

    feat_copy.wait_recv()
    for t in range(TILES):
        for half, ref in ((0, feat), (1, fx)):
            value = ref[rows(t), :] * mask(t)
            hi, lo = split(value)
            f_hi[rows(t), half * 128:(half + 1) * 128] = hi
            f_lo[rows(t), half * 128:(half + 1) * 128] = lo

    def mixed(k):
        for t in range(0, ROWS, 256):
            at = pl.ds(t, 256)
            r = dot(f_hi[at, :], w_hl[k])
            u[k, at, :] = r[:, 0:128] + r[:, 128:256] + dot(f_lo[at, :], w_hl[k, :, 0:128])

    mixed(3)
    start(halo_f(0, u.at[3]))
    for t in range(TILES):
        for j in range(3):
            hi, lo = split(blocks[t, j])
            bb[t, 0:128, j * 128:(j + 1) * 128] = hi
            bb[t, 128:256, j * 128:(j + 1) * 128] = lo
    for t in range(TILES):
        put_ext(t, u[3, rows(t), :])
        for half, ref in ((0, feat), (1, fx)):
            hi, lo = split((ref[rows(t), :] * mask(t)).T)
            ft_hi[half * 128:(half + 1) * 128, t * 128:(t + 1) * 128] = hi
            ft_lo[half * 128:(half + 1) * 128, t * 128:(t + 1) * 128] = lo

    finish_s(0)
    spread(1)
    wg_partial(0)
    mixed(2)

    halo_in(0)
    for t in range(TILES):
        b[0, rows(t), :] = u[2, rows(t), :] + 2.0 * apply(t)
    start(halo_f(1, b.at[0]))
    for t in range(TILES):
        put_ext(t, b[0, rows(t), :])
    wg_partial(1)
    wg_lat(0)
    mixed(1)

    finish_s(1)
    spread(2)
    wg_lat(1)
    wg_lon(0)
    wg_partial(2)

    halo_in(1)
    for t in range(TILES):
        b[1, rows(t), :] = u[1, rows(t), :] + 2.0 * apply(t) - u[3, rows(t), :]
    start(halo_f(2, b.at[1]))
    for t in range(TILES):
        put_ext(t, b[1, rows(t), :])
    for t in range(TILES):
        r = ig_term(0, t) + ig_term(1, t) + ig_term(2, t)
        ig_acc[rows(t), :] = r[:, 0:128]
        ig_send[0, rows(t), :] = r[:, 128:256]
    ig_copy(0).start()
    wg_lon(1)
    wg_lat(2)
    wg_back(0)

    finish_s(2)
    wg_partial(3)
    for t in range(TILES):
        r = ig_term(3, t)
        ig_acc[rows(t), :] += r[:, 0:128]
        ig_send[1, rows(t), :] = r[:, 128:256]
    ig_copy(1).start()
    wg_lon(2)
    wg_back(1)
    mixed(0)
    wg_lat(3)

    halo_in(2)
    for t in range(TILES):
        out[rows(t), :] = u[0, rows(t), :] + apply(t) - b[0, rows(t), :]
    wg_lon(3)
    wg_back(2)
    ig_copy(0).wait_recv()
    ig_copy(1).wait_recv()
    for t in range(TILES):
        at = rows(t)
        ig[at, :] = (ig_acc[at, :] + (ig_recv[0, at, :] + ig_recv[1, at, :])) * mask(t)
    wg_back(3)
    for k in range(CHEB):
        wg_done(k)

    feat_copy.wait_send()
    for i in range(3):
        sent(halo_f(i, (u.at[3], b.at[0], b.at[1])[i]))
        sent(halo_s(i))
    ig_copy(0).wait_send()
    ig_copy(1).wait_send()
    for k in range(CHEB):
        wg_sent(k)


def shards(n_lon, n_lat, features, blocks, sources, live, weights, cotangent):
    own_lon = min(n_lon, 256 // n_lat // 8)
    part = 256 // n_lat
    piece = part // own_lon
    scale = float(ROWS * n_lon * n_lat) ** (-0.5)
    vmem = pl.BlockSpec(memory_space=pltpu.VMEM)
    smem = pl.BlockSpec(memory_space=pltpu.SMEM)
    dma = pltpu.SemaphoreType.DMA
    lons, lats = max(n_lon - 1, 1), max(n_lat - 1, 1)
    return pl.pallas_call(
        functools.partial(kernel, n_lon, n_lat, own_lon, scale),
        out_shape=(
            jax.ShapeDtypeStruct((ROWS, 128), F32),
            jax.ShapeDtypeStruct((ROWS, 128), F32),
            jax.ShapeDtypeStruct((CHEB, 256, 128), F32),
        ),
        in_specs=[vmem, vmem, smem, smem, vmem, vmem],
        out_specs=(vmem, vmem, vmem),
        scratch_shapes=[
            pltpu.VMEM((ROWS, 128), F32),
            pltpu.VMEM((ROWS, 256), BF16),
            pltpu.VMEM((ROWS, 256), BF16),
            pltpu.VMEM((256, ROWS), BF16),
            pltpu.VMEM((256, ROWS), BF16),
            pltpu.VMEM((CHEB, 256, 256), BF16),
            pltpu.VMEM((CHEB, 256, 256), BF16),
            pltpu.VMEM((CHEB, 128, 256), BF16),
            pltpu.VMEM((TILES, 256, 384), BF16),
            pltpu.VMEM((TILES, 384, 256), BF16),
            pltpu.VMEM((CHEB, ROWS, 128), F32),
            pltpu.VMEM((2, ROWS, 128), F32),
            pltpu.VMEM((CHEB, ROWS, 128), F32),
            pltpu.VMEM((CHEB, ROWS, 256), BF16),
            pltpu.VMEM((TILES + 4, 128, 256), BF16),
            pltpu.VMEM((TILES + 4, 128, 128), F32),
            pltpu.VMEM((8, 128, 128), F32),
            pltpu.VMEM((3, 4, 128, 128), F32),
            pltpu.VMEM((3, 4, 128, 128), F32),
            pltpu.VMEM((3, 4, 128, 128), F32),
            pltpu.VMEM((ROWS, 128), F32),
            pltpu.VMEM((2, ROWS, 128), F32),
            pltpu.VMEM((2, ROWS, 128), F32),
            pltpu.VMEM((CHEB, 256, 128), F32),
            pltpu.VMEM((CHEB, lats, part, 128), F32),
            pltpu.VMEM((CHEB, part, 128), F32),
            pltpu.VMEM((CHEB, lons, piece, 128), F32),
            pltpu.VMEM((CHEB, 256, 128), F32),
            dma((2,)),
            dma((3, 4)), dma((3, 4)),
            dma((3, 4)), dma((3, 4)),
            dma((2,)), dma((2,)),
            dma((CHEB, lats)), dma((CHEB, lats)),
            dma((CHEB, lons)), dma((CHEB, lons)),
            dma((CHEB, lons)), dma((CHEB, lons)),
            dma((CHEB, lats)), dma((CHEB, lats)),
        ],
        compiler_params=pltpu.CompilerParams(
            collective_id=0, has_side_effects=True, vmem_limit_bytes=48 * 1024 * 1024
        ),
        cost_estimate=pl.CostEstimate(flops=3_200_000_000, bytes_accessed=4_200_000, transcendentals=0),
    )(features, blocks, sources, live, weights, cotangent)


def solution(mesh):
    placed = (
        P(("groups", "lon", "lat"), "ch"),
        P(("lon", "lat"), None, None, None),
        P(("lon", "lat"), None),
        P(("lon", "lat")),
        P(None, None, "ch"),
        P(("groups", "lon", "lat"), "ch"),
    )
    return jax.shard_map(
        functools.partial(shards, mesh.shape["lon"], mesh.shape["lat"]),
        mesh=mesh,
        in_specs=placed,
        out_specs=(
            P(("groups", "lon", "lat"), "ch"),
            P(("groups", "lon", "lat"), "ch"),
            P("groups", None, "ch"),
        ),
        check_vma=False,
    )
```

```python
import functools

import jax
import jax.numpy as jnp
from jax import lax
from jax.experimental import pallas as pl
from jax.experimental.pallas import tpu as pltpu
from jax.sharding import PartitionSpec as P

CHEB = 4
TILE = 128
TILES = 6
ROWS = TILE * TILES
MESH = pl.DeviceIdType.MESH
F32 = jnp.float32
BF16 = jnp.bfloat16


def dot(a, b):
    return jnp.dot(a, b, preferred_element_type=F32)


def split(x):
    hi = x.astype(BF16)
    return hi, (x - hi.astype(F32)).astype(BF16)


def kernel(
    n_lon, n_lat, own_lon, scale,
    feat_in, blocks_in, src, live, w_in, cot_in,
    out, ig, wg,
    feat, blocks, w, cot, in_sem,
    tx, t_hl, ft_hi, ft_lo, w_hl, wt_hh, wt_lo, bb, bt,
    term, mix, s, s_hl, ext, loc, free, sp,
    recv_f, recv_s, ig_acc, ig_send, ig_recv,
    wg_part, rx, wg_x, rz, wg_sum,
    tx_send, tx_recv, hf_send, hf_recv, hs_send, hs_recv, ig_ssem, ig_rsem,
    rx_send, rx_recv, rz_send, rz_recv, az_send, az_recv, ax_send, ax_recv,
):
    part = 256 // n_lat
    piece = part // own_lon
    ch = lax.axis_index("ch")
    lon = lax.axis_index("lon")
    lat = lax.axis_index("lat")
    west = lax.rem(lon + n_lon - 1, n_lon)
    east = lax.rem(lon + 1, n_lon)
    mine = pl.ds(pl.multiple_of(ch * 128, 128), 128)
    other = pl.ds(pl.multiple_of((1 - ch) * 128, 128), 128)

    def rows(t):
        return pl.ds(t * TILE, TILE)

    def mask(t):
        return (t < live[0]).astype(F32)

    def remote(a, d, ssem, rsem, dev):
        return pltpu.make_async_remote_copy(
            src_ref=a, dst_ref=d, send_sem=ssem, recv_sem=rsem, device_id=dev, device_id_type=MESH
        )

    inputs = [
        pltpu.make_async_copy(a, d, in_sem.at[i])
        for i, (a, d) in enumerate(((blocks_in, blocks), (cot_in, cot), (w_in, w), (feat_in, feat)))
    ]
    for copy in inputs:
        copy.start()

    barrier = pltpu.get_barrier_semaphore()
    pl.semaphore_signal(barrier, inc=1, device_id={"ch": 1 - ch}, device_id_type=MESH)
    for d in range(1, n_lat):
        pl.semaphore_signal(barrier, inc=1, device_id={"lat": lax.rem(lat + d, n_lat)}, device_id_type=MESH)

    @pl.loop(1, n_lon)
    def _(d):
        pl.semaphore_signal(barrier, inc=1, device_id={"lon": lax.rem(lon + d, n_lon)}, device_id_type=MESH)

    has_south = lat > 0
    has_north = lat < n_lat - 1

    def halo_f(i, v):
        return (
            (None, remote(v.at[rows(1)], recv_f.at[i, 0], hf_send.at[i, 0], hf_recv.at[i, 0], {"lon": east})),
            (None, remote(v.at[rows(0)], recv_f.at[i, 1], hf_send.at[i, 1], hf_recv.at[i, 1], {"lon": west})),
            (has_north, remote(v.at[rows(3)], recv_f.at[i, 2], hf_send.at[i, 2], hf_recv.at[i, 2], {"lat": lat + 1})),
            (has_south, remote(v.at[rows(2)], recv_f.at[i, 3], hf_send.at[i, 3], hf_recv.at[i, 3], {"lat": lat - 1})),
        )

    def halo_s(i):
        return (
            (None, remote(sp.at[i, 0], recv_s.at[i, 1], hs_send.at[i, 0], hs_recv.at[i, 1], {"lon": west})),
            (None, remote(sp.at[i, 1], recv_s.at[i, 0], hs_send.at[i, 1], hs_recv.at[i, 0], {"lon": east})),
            (has_south, remote(sp.at[i, 2], recv_s.at[i, 3], hs_send.at[i, 2], hs_recv.at[i, 3], {"lat": lat - 1})),
            (has_north, remote(sp.at[i, 3], recv_s.at[i, 2], hs_send.at[i, 3], hs_recv.at[i, 2], {"lat": lat + 1})),
        )

    def on(condition, action):
        if condition is None:
            action()
        else:
            pl.when(condition)(action)

    def start(copies):
        for condition, copy in copies:
            on(condition, copy.start)

    def sent(copies):
        for condition, copy in copies:
            on(condition, copy.wait_send)

    def landed(i, buffer, sems):
        for j, condition in ((0, None), (1, None), (2, has_south), (3, has_north)):
            at = buffer.at[i, j]
            on(condition, remote(at, at, hf_send.at[i, j], sems.at[i, j], {"lon": east}).wait_recv)

    def put_s(k, t, value):
        s[k, rows(t), :] = value
        hi, lo = split(value)
        s_hl[k, rows(t), 0:128] = hi
        s_hl[k, rows(t), 128:256] = lo

    def spread(i):
        for t in range(TILES):
            a = s_hl[i, rows(t), :]
            low = jnp.concatenate([a[:, 0:128], jnp.zeros((128, 128), BF16)], axis=1)
            r = dot(bt[t], jnp.concatenate([a, low], axis=0))
            share = r[:, 0:128] + r[:, 128:256]
            loc[t] = share[0:128]
            if t < 4:
                loc[6 + t] = share[128:256]
            else:
                free[2 + t] = share[128:256]
            free[t] = share[256:384]

        def gathered(e):
            total = loc[e]
            for f in range(8):
                entry = src[2, f] if f < 6 else src[1, f - 2]
                total = total + (entry == e).astype(F32) * free[f]
            return total

        @pl.loop(6, 10)
        def _(e):
            sp[i, e - 6] = gathered(e)

        start(halo_s(i))

        @pl.loop(0, 6)
        def _(e):
            loc[e] = gathered(e)

    def finish_s(i):
        landed(i, recv_s, hs_recv)
        for t in range(TILES):
            total = loc[t]
            if t < 4:
                total = total + recv_s[i, t]
            total = total * mask(t)
            if i > 0:
                total = 2.0 * total - s[i - 1, rows(t), :]
            put_s(i + 1, t, total)

    def put_ext(t, value):
        hi, lo = split(value)
        ext[t, :, 0:128] = hi
        ext[t, :, 128:256] = lo

    def put_split(k, t):
        hi, lo = split(term[k, rows(t), :])
        t_hl[k, 0, rows(t), 0:128] = hi
        t_hl[k, 1, rows(t), 0:128] = lo
        if k < CHEB - 1:
            ext[t, :, 0:128] = hi
            ext[t, :, 128:256] = lo

    def term_copy(k):
        a = feat_in if k == 0 else term.at[k]
        return remote(a, tx.at[k], tx_send.at[k], tx_recv.at[k], {"ch": 1 - ch})

    def term_in(k):
        term_copy(k).wait_recv()
        for t in range(TILES):
            value = tx[k, rows(t), :]
            if k == 0:
                value = value * mask(t)
            hi, lo = split(value)
            t_hl[k, 0, rows(t), 128:256] = hi
            t_hl[k, 1, rows(t), 128:256] = lo
            if k < 2:
                for side, x in ((0, term[k, rows(t), :]), (1, value)):
                    hi, lo = split(x.T)
                    ft_hi[k, side * 128:(side + 1) * 128, t * 128:(t + 1) * 128] = hi
                    ft_lo[k, side * 128:(side + 1) * 128, t * 128:(t + 1) * 128] = lo

    def mixed(k):
        for t in range(0, ROWS, 256):
            at = pl.ds(t, 256)
            r = dot(t_hl[k, 0, at, :], w_hl[k])
            r = r[:, 0:128] + r[:, 128:256] + dot(t_hl[k, 1, at, :], w_hl[k, :, 0:128])
            if k == CHEB - 1:
                out[at, :] = mix[at, :] + r
            elif k == 0:
                mix[at, :] = r
            else:
                mix[at, :] += r

    def apply(t):
        x = jnp.concatenate([ext[src[0, t]], ext[src[1, t]], ext[src[2, t]]], axis=0)
        r = dot(bb[t], x)
        return (r[0:128, 0:128] + (r[0:128, 128:256] + r[128:256, 0:128])) * mask(t)

    def halo_in(i):
        landed(i, recv_f, hf_recv)
        for j in range(4):
            put_ext(6 + j, recv_f[i, j])

    def next_term(i):
        halo_in(i)
        for t in range(TILES):
            total = apply(t)
            if i > 0:
                total = 2.0 * total - term[i - 1, rows(t), :]
            term[i + 1, rows(t), :] = total
        if i < 2:
            start(halo_f(i + 1, term.at[i + 1]))
        term_copy(i + 1).start()
        for t in range(TILES):
            put_split(i + 1, t)

    def wg_partial(k):
        first, second = (0, k) if k < 2 else (1, k - 1)
        a = s_hl[second]
        r = dot(ft_hi[first], a)
        r = (r[:, 0:128] + r[:, 128:256] + dot(ft_lo[first], a[:, 0:128])) * scale
        for half, at in ((0, mine), (1, other)):
            value = r[half * 128:(half + 1) * 128]
            if k >= 2:
                value = 2.0 * value - wg_part[k - 2, at, :]
            wg_part[k, at, :] = value
        for d in range(1, n_lat):
            x_copy(k, d).start()

    def part_of(index):
        return pl.ds(pl.multiple_of(index * part, 8), part)

    def piece_of(index):
        return pl.ds(pl.multiple_of(index * piece, 8), piece)

    def x_copy(k, d):
        to = lax.rem(lat + d, n_lat)
        return remote(wg_part.at[k, part_of(to)], rx.at[k, d - 1], rx_send.at[k, d - 1], rx_recv.at[k, d - 1], {"lat": to})

    def z_copy(k, d):
        to = lax.rem(lon + d, n_lon)
        return to, remote(wg_x.at[k, piece_of(to)], rz.at[k, d - 1], rz_send.at[k, d - 1], rz_recv.at[k, d - 1], {"lon": to})

    def final_piece(k, owner):
        return wg_sum.at[k, pl.ds(pl.multiple_of(lat * part + owner * piece, 8), piece)]

    def az_copy(k, d):
        at = final_piece(k, lon)
        return remote(at, at, az_send.at[k, d - 1], az_recv.at[k, d - 1], {"lon": lax.rem(lon + d, n_lon)})

    def ax_copy(k, d):
        at = wg_sum.at[k, part_of(lat)]
        return remote(at, at, ax_send.at[k, d - 1], ax_recv.at[k, d - 1], {"lat": lax.rem(lat + d, n_lat)})

    def each_lon(body):
        if n_lon <= 4:
            for d in range(1, n_lon):
                body(d)
        else:
            pl.loop(1, n_lon)(body)

    everyone = own_lon == n_lon
    is_owner = None if everyone else lon < own_lon

    def owner_only(index, action):
        on(None if everyone else index < own_lon, action)

    def wg_lat(k):
        total = wg_part[k, part_of(lat), :]
        for d in range(1, n_lat):
            x_copy(k, d).wait_recv()
            total = total + rx[k, d - 1]
        wg_x[k] = total

        def send(d):
            to, copy = z_copy(k, d)
            owner_only(to, copy.start)

        each_lon(send)

    def wg_lon(k):
        def total_up():
            each_lon(lambda d: z_copy(k, d)[1].wait_recv())
            total = wg_x[k, piece_of(lon), :]
            if n_lon <= 4:
                for d in range(1, n_lon):
                    total = total + rz[k, d - 1]
            else:
                total = lax.fori_loop(1, n_lon, lambda d, t: t + rz[k, d - 1], total)
            wg_sum[k, pl.ds(pl.multiple_of(lat * part + lon * piece, 8), piece), :] = total
            each_lon(lambda d: az_copy(k, d).start())

        on(is_owner, total_up)

    def wg_back(k):
        def take(d):
            owner = lax.rem(lon + n_lon - d, n_lon)

            def wait():
                at = final_piece(k, owner)
                remote(at, at, az_send.at[k, d - 1], az_recv.at[k, d - 1], {"lon": east}).wait_recv()

            owner_only(owner, wait)

        each_lon(take)
        for d in range(1, n_lat):
            ax_copy(k, d).start()

    def wg_done(k):
        for d in range(1, n_lat):
            at = wg_sum.at[k, part_of(lax.rem(lat + n_lat - d, n_lat))]
            remote(at, at, ax_send.at[k, d - 1], ax_recv.at[k, d - 1], {"lon": east}).wait_recv()
        wg[k] = wg_sum[k]

    def wg_sent(k):
        for d in range(1, n_lat):
            x_copy(k, d).wait_send()
            ax_copy(k, d).wait_send()

        def wait(d):
            to, copy = z_copy(k, d)
            owner_only(to, copy.wait_send)

        each_lon(wait)
        on(is_owner, lambda: each_lon(lambda d: az_copy(k, d).wait_send()))

    def ig_copy(i):
        return remote(ig_send.at[i], ig_recv.at[i], ig_ssem.at[i], ig_rsem.at[i], {"ch": 1 - ch})

    def ig_term(k, t):
        a = s_hl[k, rows(t), :]
        return dot(a, wt_hh[k]) + dot(a[:, 0:128], wt_lo[k])

    @pl.when(jnp.logical_not(has_south))
    def _():
        for i in range(3):
            recv_f[i, 2] = jnp.zeros((128, 128), F32)
            recv_s[i, 2] = jnp.zeros((128, 128), F32)

    @pl.when(jnp.logical_not(has_north))
    def _():
        for i in range(3):
            recv_f[i, 3] = jnp.zeros((128, 128), F32)
            recv_s[i, 3] = jnp.zeros((128, 128), F32)

    pl.semaphore_wait(barrier, (n_lat - 1) + (n_lon - 1) + 1)
    start(halo_f(0, feat_in))
    term_copy(0).start()

    inputs[0].wait()
    inputs[1].wait()
    for t in range(TILES):
        for j in range(3):
            hi, lo = split(blocks[t, j].T)
            bt[t, j * 128:(j + 1) * 128, 0:128] = hi
            bt[t, j * 128:(j + 1) * 128, 128:256] = lo
        put_s(0, t, cot[rows(t), :] * mask(t))
    spread(0)

    inputs[2].wait()
    inputs[3].wait()
    for t in range(TILES):
        for j in range(3):
            hi, lo = split(blocks[t, j])
            bb[t, 0:128, j * 128:(j + 1) * 128] = hi
            bb[t, 128:256, j * 128:(j + 1) * 128] = lo
        term[0, rows(t), :] = feat[rows(t), :] * mask(t)
        put_split(0, t)

    next_term(0)
    term_in(0)
    wg_partial(0)

    finish_s(0)
    spread(1)
    wg_partial(1)
    term_in(1)
    wg_partial(2)
    wg_lat(0)
    for k in range(CHEB):
        for side, at in ((0, mine), (1, other)):
            value = w[k, at, :]
            hi, lo = split(value)
            w_hl[k, side * 128:(side + 1) * 128, 0:128] = hi
            w_hl[k, side * 128:(side + 1) * 128, 128:256] = lo
            hi, lo = split(value.T)
            wt_hh[k, 0:128, side * 128:(side + 1) * 128] = hi
            wt_hh[k, 128:256, side * 128:(side + 1) * 128] = hi
            wt_lo[k, :, side * 128:(side + 1) * 128] = lo

    next_term(1)
    wg_lat(1)
    wg_lat(2)
    wg_lon(0)
    mixed(0)
    mixed(1)

    finish_s(1)
    spread(2)
    wg_partial(3)
    wg_lon(1)
    wg_lon(2)
    wg_back(0)
    term_in(2)
    mixed(2)
    for t in range(TILES):
        r = ig_term(0, t) + ig_term(1, t) + ig_term(2, t)
        ig_acc[rows(t), :] = r[:, 0:128]
        ig_send[0, rows(t), :] = r[:, 128:256]
    ig_copy(0).start()
    wg_lat(3)

    next_term(2)
    wg_lon(3)
    wg_back(1)
    wg_back(2)

    finish_s(2)
    for t in range(TILES):
        r = ig_term(3, t)
        ig_acc[rows(t), :] += r[:, 0:128]
        ig_send[1, rows(t), :] = r[:, 128:256]
    ig_copy(1).start()
    wg_back(3)
    term_in(3)
    mixed(3)
    ig_copy(0).wait_recv()
    ig_copy(1).wait_recv()
    for t in range(TILES):
        at = rows(t)
        ig[at, :] = (ig_acc[at, :] + (ig_recv[0, at, :] + ig_recv[1, at, :])) * mask(t)
    for k in range(CHEB):
        wg_done(k)

    for i in range(3):
        sent(halo_f(i, feat_in if i == 0 else term.at[i]))
        sent(halo_s(i))
    ig_copy(0).wait_send()
    ig_copy(1).wait_send()
    for k in range(CHEB):
        term_copy(k).wait_send()
        wg_sent(k)


def write_out(a, b, c, a_out, b_out, c_out, sem):
    copies = [
        pltpu.make_async_copy(x, y, sem.at[i]) for i, (x, y) in enumerate(((a, a_out), (b, b_out), (c, c_out)))
    ]
    for copy in copies:
        copy.start()
    for copy in copies:
        copy.wait()


def shards(n_lon, n_lat, features, blocks, sources, live, weights, cotangent):
    own_lon = min(n_lon, 256 // n_lat // 8)
    part = 256 // n_lat
    piece = part // own_lon
    scale = float(ROWS * n_lon * n_lat) ** (-0.5)
    vmem = pl.BlockSpec(memory_space=pltpu.VMEM)
    smem = pl.BlockSpec(memory_space=pltpu.SMEM)
    dma = pltpu.SemaphoreType.DMA
    lons, lats = max(n_lon - 1, 1), max(n_lat - 1, 1)
    hbm = pl.BlockSpec(memory_space=pltpu.HBM)
    results = pl.pallas_call(
        functools.partial(kernel, n_lon, n_lat, own_lon, scale),
        out_shape=(
            jax.ShapeDtypeStruct((ROWS, 128), F32),
            jax.ShapeDtypeStruct((ROWS, 128), F32),
            jax.ShapeDtypeStruct((CHEB, 256, 128), F32),
        ),
        in_specs=[hbm, hbm, smem, smem, hbm, hbm],
        out_specs=(vmem, vmem, vmem),
        scratch_shapes=[
            pltpu.VMEM((ROWS, 128), F32),
            pltpu.VMEM((TILES, 3, 128, 128), F32),
            pltpu.VMEM((CHEB, 256, 128), F32),
            pltpu.VMEM((ROWS, 128), F32),
            dma((4,)),
            pltpu.VMEM((CHEB, ROWS, 128), F32),
            pltpu.VMEM((CHEB, 2, ROWS, 256), BF16),
            pltpu.VMEM((2, 256, ROWS), BF16),
            pltpu.VMEM((2, 256, ROWS), BF16),
            pltpu.VMEM((CHEB, 256, 256), BF16),
            pltpu.VMEM((CHEB, 256, 256), BF16),
            pltpu.VMEM((CHEB, 128, 256), BF16),
            pltpu.VMEM((TILES, 256, 384), BF16),
            pltpu.VMEM((TILES, 384, 256), BF16),
            pltpu.VMEM((CHEB, ROWS, 128), F32),
            pltpu.VMEM((ROWS, 128), F32),
            pltpu.VMEM((CHEB, ROWS, 128), F32),
            pltpu.VMEM((CHEB, ROWS, 256), BF16),
            pltpu.VMEM((TILES + 4, 128, 256), BF16),
            pltpu.VMEM((TILES + 4, 128, 128), F32),
            pltpu.VMEM((8, 128, 128), F32),
            pltpu.VMEM((3, 4, 128, 128), F32),
            pltpu.VMEM((3, 4, 128, 128), F32),
            pltpu.VMEM((3, 4, 128, 128), F32),
            pltpu.VMEM((ROWS, 128), F32),
            pltpu.VMEM((2, ROWS, 128), F32),
            pltpu.VMEM((2, ROWS, 128), F32),
            pltpu.VMEM((CHEB, 256, 128), F32),
            pltpu.VMEM((CHEB, lats, part, 128), F32),
            pltpu.VMEM((CHEB, part, 128), F32),
            pltpu.VMEM((CHEB, lons, piece, 128), F32),
            pltpu.VMEM((CHEB, 256, 128), F32),
            dma((CHEB,)), dma((CHEB,)),
            dma((3, 4)), dma((3, 4)),
            dma((3, 4)), dma((3, 4)),
            dma((2,)), dma((2,)),
            dma((CHEB, lats)), dma((CHEB, lats)),
            dma((CHEB, lons)), dma((CHEB, lons)),
            dma((CHEB, lons)), dma((CHEB, lons)),
            dma((CHEB, lats)), dma((CHEB, lats)),
        ],
        compiler_params=pltpu.CompilerParams(
            collective_id=0, has_side_effects=True, vmem_limit_bytes=60 * 1024 * 1024
        ),
        cost_estimate=pl.CostEstimate(flops=3_200_000_000, bytes_accessed=4_200_000, transcendentals=0),
    )(features, blocks, sources.T, live, weights, cotangent)
    return pl.pallas_call(
        write_out,
        out_shape=tuple(jax.ShapeDtypeStruct(a.shape, a.dtype) for a in results),
        in_specs=[vmem] * 3,
        out_specs=(hbm,) * 3,
        scratch_shapes=[dma((3,))],
        cost_estimate=pl.CostEstimate(flops=0, bytes_accessed=2_600_000, transcendentals=0),
    )(*results)


def solution(mesh):
    placed = (
        P(("groups", "lon", "lat"), "ch"),
        P(("lon", "lat"), None, None, None),
        P(("lon", "lat"), None),
        P(("lon", "lat")),
        P(None, None, "ch"),
        P(("groups", "lon", "lat"), "ch"),
    )
    return jax.shard_map(
        functools.partial(shards, mesh.shape["lon"], mesh.shape["lat"]),
        mesh=mesh,
        in_specs=placed,
        out_specs=(
            P(("groups", "lon", "lat"), "ch"),
            P(("groups", "lon", "lat"), "ch"),
            P("groups", None, "ch"),
        ),
        check_vma=False,
    )
```
